32 devices in a mesh: row: 4 (over x, core), col: 8 (over z, y).
Axes of the slice: x: 2, y: 2, z: 4, core: 2. Of those that a mesh axis runs over, the one named last changes fastest.
Arguments:
- velocity: float32 [3, 1536, 32, 1536], P(None, 'col', None, 'row'), may hold values from -6 to 6
- wall_operator: bfloat16 [1536, 1536], replicated, may hold values from -0.15625 to 0.15625
- span_operator: bfloat16 [1536, 1536], replicated, may hold values from -0.15625 to 0.15625
Outputs:
- convection: float32 [3, 1536, 32, 1536], P(None, 'col', None, 'row')
The draws below stay inside these ranges and needn't reach their ends.
All inputs are finite; a program needn't handle non-finite values.
Results may differ from the reference program's by a relative error of at most 0.0053.
Values may be sent and summed in bfloat16 or wider, within the bound.
A program may use at most 320 MiB of HBM per device.

```python
import jax
import jax.numpy as jnp
from jax import lax

NY = 1536
NZ = 1536
XS = 32


def level_of(stream_key, shape, pieces, least, top_value):
    def one(position, shards_of):
        steps = jax.random.uniform(jax.random.fold_in(jax.random.fold_in(stream_key, 6), position), (shards_of,), jnp.float32, least / len(pieces), top_value / len(pieces))
        return jnp.repeat(jnp.exp(steps), shape[position] // shards_of).reshape((-1,) + (1,) * (len(shape) - position - 1))

    gain = one(*pieces[0])
    for cut in pieces[1:]:
        gain = gain * one(*cut)
    return gain


def bell_draw(own_key, dims, spread, bound, split=(), held_as=jnp.bfloat16):
    values = spread * jax.random.normal(own_key, dims, jnp.float32)
    if split:
        values = values * level_of(own_key, dims, split, -0.22, 0.18)
    return jnp.clip(values, -bound, bound).astype(held_as)


def setup_inputs(seed: int = 0) -> dict:
    keys = jax.random.split(jax.random.key(seed), 4)
    velocity = bell_draw(keys[0], (3, NZ, XS, NY), 1.0, 6.0, ((1, 8), (3, 4)), jnp.float32)
    wall_operator = bell_draw(keys[1], (NY, NY), NY ** -0.5, 0.15625)
    span_operator = bell_draw(keys[2], (NZ, NZ), NZ ** -0.5, 0.15625)
    return dict(velocity=velocity, wall_operator=wall_operator, span_operator=span_operator)


def axial_share_entry(truncated_outcome, slope_operator_grid, holder_slot_index, transpose_arrangement):
    promoted_operand = lax.optimization_barrier(truncated_outcome).astype(jnp.float32)
    speed_field_holder = promoted_operand[holder_slot_index]
    speed_pair_flux = lax.optimization_barrier((promoted_operand * speed_field_holder).astype(jnp.bfloat16)).astype(jnp.float32)
    stacked = jnp.concatenate([promoted_operand, speed_pair_flux], 0)
    gradient_entries = jnp.einsum(transpose_arrangement, stacked, slope_operator_grid.astype(jnp.float32), precision=lax.Precision.HIGHEST)
    return 0.5 * (gradient_entries[3:] + speed_field_holder * gradient_entries[:3])


def reference(velocity, wall_operator, span_operator):
    def plane_terms(plane_index):
        plane_values = lax.dynamic_index_in_dim(velocity, plane_index, 2, keepdims=False)
        truncated_outcome = plane_values.astype(jnp.bfloat16)
        wall_part = axial_share_entry(truncated_outcome, wall_operator, 1, "fzy,Yy->fzY")
        span_part = axial_share_entry(truncated_outcome, span_operator, 2, "fzy,Zz->fZy")
        return wall_part + span_part

    planes = lax.map(plane_terms, jnp.arange(XS, dtype=jnp.int32))
    return jnp.moveaxis(planes, 0, 2)
```

```python
import functools

import jax
import jax.numpy as jnp
from jax import lax
from jax.experimental import pallas as pl
from jax.experimental.pallas import tpu as pltpu
from jax.sharding import PartitionSpec as P

MESH = pl.DeviceIdType.MESH


def exchange_kernel(
    nrow, ncol, yl,
    lines, wall_t, span_op,
    row_in, col_in, wall_back, span_back,
    wslot, lhs, wout, sslot, prod, sout,
    row_send, row_recv, col_send, col_recv, wb_send, wb_recv, sb_send, sb_recv, load_sem,
):
    my_row, my_col = lax.axis_index("row"), lax.axis_index("col")
    xs, zl = lines.shape[0], lines.shape[1]
    nz = span_op.shape[0]
    pr, pc = xs // nrow, xs // ncol
    f32, bf16 = jnp.float32, jnp.bfloat16

    def row_peer(k):
        return lax.rem(my_row + k, nrow)

    def col_peer(k):
        return lax.rem(my_col + k, ncol)

    def zrows(index):
        return pl.ds(pl.multiple_of(index * zl, 16), zl)

    def move(src, dst, send, recv, axis, k):
        if k == 0:
            return pltpu.make_async_copy(src, dst, recv)
        peer = row_peer(k) if axis == "row" else col_peer(k)
        return pltpu.make_async_remote_copy(
            src_ref=src, dst_ref=dst, send_sem=send, recv_sem=recv,
            device_id={axis: peer}, device_id_type=MESH,
        )

    def row_copy(p, k):
        return move(
            lines.at[row_peer(k) * pr + p], row_in.at[p, my_row],
            row_send.at[p, k], row_recv.at[p, k], "row", k,
        )

    def col_copy(p, k):
        return move(
            lines.at[col_peer(k) * pc + p], col_in.at[p, zrows(my_col)],
            col_send.at[p, k], col_recv.at[p, k], "col", k,
        )

    def wall_copy(p, k):
        return move(
            wout.at[p, row_peer(k)], wall_back.at[my_row * pr + p],
            wb_send.at[p, k], wb_recv.at[p, k], "row", k,
        )

    def span_copy(p, k):
        return move(
            sout.at[p, zrows(col_peer(k))], span_back.at[my_col * pc + p],
            sb_send.at[p, k], sb_recv.at[p, k], "col", k,
        )

    def arrived(copy, k):
        if k == 0:
            copy.wait()
        else:
            copy.wait_recv()

    barrier = pltpu.get_barrier_semaphore()
    for k in range(1, nrow):
        pl.semaphore_signal(barrier, inc=1, device_id={"row": row_peer(k)}, device_id_type=MESH)
    for k in range(1, ncol):
        pl.semaphore_signal(barrier, inc=1, device_id={"col": col_peer(k)}, device_id_type=MESH)
    pl.semaphore_wait(barrier, nrow + ncol - 2)

    per = pr // pc

    def launch(i, carry):
        for k in list(range(1, ncol)) + [0]:
            col_copy(i, k).start()

        def launch_row(j, inner):
            for k in list(range(1, nrow)) + [0]:
                row_copy(i * per + j, k).start()
            return inner

        return lax.fori_loop(0, per, launch_row, carry)

    lax.fori_loop(0, pc, launch, 0)

    def wall_plane(p):
        for k in range(nrow):
            arrived(row_copy(p, k), k)
        load = pltpu.make_async_copy(row_in.at[p], wslot, load_sem.at[0])
        load.start()
        load.wait()
        for b in range(nrow):
            speed = wslot[b, :, yl : 2 * yl].astype(f32)
            for c in range(3):
                field = wslot[b, :, c * yl : (c + 1) * yl]
                lhs[c, :zl, b * yl : (b + 1) * yl] = field
                lhs[c, zl:, b * yl : (b + 1) * yl] = (field.astype(f32) * speed).astype(bf16)

        def component(c, carry):
            for h in range(0, nrow, 2):
                acc = jnp.dot(
                    lhs[c], wall_t[:, h * yl : (h + 2) * yl], preferred_element_type=f32
                )
                for b in (0, 1):
                    speed = wslot[h + b, :, yl : 2 * yl].astype(f32)
                    part = acc[:, b * yl : (b + 1) * yl]
                    wout[p, h + b, :, pl.ds(pl.multiple_of(c * yl, 128), yl)] = (
                        0.5 * (part[zl:] + speed * part[:zl])
                    ).astype(bf16)
            return carry

        lax.fori_loop(0, 3, component, 0)
        for k in list(range(1, nrow)) + [0]:
            wall_copy(p, k).start()

    tile = nz // 4

    def span_plane(p):
        for k in range(ncol):
            arrived(col_copy(p, k), k)
        load = pltpu.make_async_copy(col_in.at[p], sslot, load_sem.at[1])
        load.start()
        load.wait()

        def products(t, carry):
            rows = pl.ds(pl.multiple_of(t * tile, 16), tile)
            speed = sslot[rows, 2 * yl : 3 * yl].astype(f32)
            for c in range(3):
                cells = slice(c * yl, (c + 1) * yl)
                prod[rows, cells] = (sslot[rows, cells].astype(f32) * speed).astype(bf16)
            return carry

        lax.fori_loop(0, 4, products, 0)

        def outputs(t, carry):
            rows = pl.ds(pl.multiple_of(t * tile, 16), tile)
            speed = sslot[rows, 2 * yl : 3 * yl].astype(f32)
            first = jnp.dot(span_op[rows, :], sslot[...], preferred_element_type=f32)
            second = jnp.dot(span_op[rows, :], prod[...], preferred_element_type=f32)
            for c in range(3):
                cells = slice(c * yl, (c + 1) * yl)
                sout[p, rows, cells] = (0.5 * (second[:, cells] + speed * first[:, cells])).astype(bf16)
            return carry

        lax.fori_loop(0, 4, outputs, 0)
        for k in list(range(1, ncol)) + [0]:
            span_copy(p, k).start()

    def work(i, carry):
        def wall_step(j, inner):
            wall_plane(i * per + j)
            return inner

        lax.fori_loop(0, per, wall_step, 0)
        span_plane(i)
        return carry

    lax.fori_loop(0, pc, work, 0)

    def finish_row(p, carry):
        for k in range(nrow):
            arrived(wall_copy(p, k), k)
            if k:
                wall_copy(p, k).wait_send()
                row_copy(p, k).wait_send()
        return carry

    def finish_col(p, carry):
        for k in range(ncol):
            arrived(span_copy(p, k), k)
            if k:
                span_copy(p, k).wait_send()
                col_copy(p, k).wait_send()
        return carry

    lax.fori_loop(0, pr, finish_row, 0)
    lax.fori_loop(0, pc, finish_col, 0)


def body(nrow, ncol, velocity, wall_operator, span_operator):
    _, zl, xs, yl = velocity.shape
    ny, nz = wall_operator.shape[0], span_operator.shape[0]
    pr, pc = xs // nrow, xs // ncol
    bf16 = jnp.bfloat16
    lines = velocity.astype(bf16).transpose(2, 1, 0, 3).reshape(xs, zl, 3 * yl)
    dma = pltpu.SemaphoreType.DMA
    anywhere = pl.BlockSpec(memory_space=pl.ANY)
    vmem = pl.BlockSpec(memory_space=pltpu.VMEM)
    flops = 2 * 6 * zl * pr * ny * ny + 2 * 6 * nz * pc * yl * nz
    _, _, wall_back, span_back = pl.pallas_call(
        functools.partial(exchange_kernel, nrow, ncol, yl),
        out_shape=[
            jax.ShapeDtypeStruct((pr, nrow, zl, 3 * yl), bf16),
            jax.ShapeDtypeStruct((pc, nz, 3 * yl), bf16),
            jax.ShapeDtypeStruct((xs, zl, 3 * yl), bf16),
            jax.ShapeDtypeStruct((xs, zl, 3 * yl), bf16),
        ],
        in_specs=[anywhere, vmem, vmem],
        out_specs=[anywhere] * 4,
        scratch_shapes=[
            pltpu.VMEM((nrow, zl, 3 * yl), bf16),
            pltpu.VMEM((3, 2 * zl, ny), bf16),
            pltpu.VMEM((pr, nrow, zl, 3 * yl), bf16),
            pltpu.VMEM((nz, 3 * yl), bf16),
            pltpu.VMEM((nz, 3 * yl), bf16),
            pltpu.VMEM((pc, nz, 3 * yl), bf16),
            dma((pr, nrow)), dma((pr, nrow)),
            dma((pc, ncol)), dma((pc, ncol)),
            dma((pr, nrow)), dma((pr, nrow)),
            dma((pc, ncol)), dma((pc, ncol)),
            dma((2,)),
        ],
        compiler_params=pltpu.CompilerParams(
            collective_id=0, has_side_effects=True, vmem_limit_bytes=60 * 2**20
        ),
        cost_estimate=pl.CostEstimate(
            flops=flops, bytes_accessed=8 * xs * zl * 3 * yl * 2, transcendentals=0
        ),
    )(lines, wall_operator.T, span_operator)
    total = wall_back.astype(jnp.float32) + span_back.astype(jnp.float32)
    return total.reshape(xs, zl, 3, yl).transpose(2, 1, 0, 3)


def solution(mesh):
    placed = (P(None, "col", None, "row"), P(), P())
    return jax.shard_map(
        functools.partial(body, mesh.shape["row"], mesh.shape["col"]),
        mesh=mesh, in_specs=placed, out_specs=P(None, "col", None, "row"), check_vma=False,
    )
```
